256 devices in a mesh: section: 8 (over z), tile: 32 (over y, x, core).
Axes of the slice: x: 4, y: 4, z: 8, core: 2. Of those that a mesh axis runs over, the one named last changes fastest.
Arguments:
- frames_in: bfloat16 [16, 192, 96, 128], P(None, None, 'tile'), may hold values from -6 to 6
- norm_gain: float32 [8, 192], P('section'), may hold values from 0.1 to 1.9
- conv_weight: bfloat16 [8, 27, 192, 192], P('section'), may hold values from -0.078125 to 0.078125
- conv_bias: float32 [8, 192], P('section'), may hold values from -0.5 to 0.5
Outputs:
- decoded: bfloat16 [16, 192, 96, 128], P('section', None, 'tile')
The draws below stay inside these ranges and needn't reach their ends.
All inputs are finite; a program needn't handle non-finite values.
Results may differ from the reference program's by a relative error of at most 0.017.
Values may be sent and summed in bfloat16 or wider, within the bound.
No kernel may reach another device: no remote copies, remote signals or barrier semaphores. Data moves between devices by JAX's collectives and lax.ppermute only.
A program may use at most 192 MiB of HBM per device.

```python
import jax
import jax.numpy as jnp
from jax import lax

C = 192
W = 128
LAYERS = 8
ROWS = 96
FRAMES = 16


def steps_of(stream_key, dims, cuts, least, high):
    loudness = 1.0
    for axis_at, parts in cuts:
        heights = jax.random.uniform(jax.random.fold_in(jax.random.fold_in(stream_key, 6), axis_at), (parts,), jnp.float32, least / len(cuts), high / len(cuts))
        loudness = loudness * jnp.repeat(jnp.exp(heights), dims[axis_at] // parts).reshape((-1,) + (1,) * (len(dims) - 1 - axis_at))
    return loudness


def normal_values(rng, shape, spread, most, shards=(), held_as=jnp.bfloat16):
    entries = spread * jax.random.normal(rng, shape, jnp.float32)
    if shards:
        entries = entries * steps_of(rng, shape, shards, -0.22, 0.18)
    return jnp.clip(entries, -most, most).astype(held_as)


def setup_inputs(seed: int = 0) -> dict:
    key_list = jax.random.split(jax.random.key(seed), 5)
    return {
        "frames_in": normal_values(key_list[0], (FRAMES, C, ROWS, W), 1.0, 6.0, ((2, 32),)),
        "norm_gain": jnp.clip(1.0 + 0.18 * jax.random.normal(key_list[1], (LAYERS, C), jnp.float32), 0.1, 1.9),
        "conv_weight": normal_values(key_list[2], (LAYERS, 27, C, C), (27 * C) ** -0.5, 0.078125, ((0, 8),)),
        "conv_bias": jnp.clip(jax.random.uniform(key_list[3], (LAYERS, C), jnp.float32, -0.5, 0.5) * steps_of(key_list[3], (LAYERS, C), ((0, 8),), -0.4, 0.0), -0.5, 0.5),
    }


def normalize_act(current, gains):
    values = current.astype(jnp.float32)
    meansq = lax.optimization_barrier(jnp.mean(values * values, axis=1, keepdims=True))
    normed = values * lax.rsqrt(meansq + 1e-06) * gains[None, :, None, None]
    return jax.nn.silu(normed).astype(jnp.bfloat16)

def causal_conv(hidden, weight, biases):
    frame_count, channels, height, breadth = hidden.shape
    padded = jnp.pad(hidden.astype(jnp.float32), ((2, 0), (0, 0), (1, 1), (1, 1)))
    summed = jnp.zeros((frame_count, weight.shape[1], height, breadth), jnp.float32)
    for time_off in range(3):
        for row_off in range(3):
            for col_off in range(3):
                piece = padded[time_off:time_off + frame_count, :, row_off:row_off + height, col_off:col_off + breadth]
                taps = weight[9 * time_off + 3 * row_off + col_off].astype(jnp.float32)
                summed = summed + jnp.einsum('oc,tcrw->torw', taps, piece)
    return summed + biases[None, :, None, None]

def reference(frames_in, norm_gain, conv_weight, conv_bias):
    current = frames_in
    for layer in range(LAYERS):
        hidden = normalize_act(current, norm_gain[layer])
        update = causal_conv(hidden, conv_weight[layer], conv_bias[layer])
        current = (current.astype(jnp.float32) + update).astype(jnp.bfloat16)
    return current
```

```python
import functools

import jax
import jax.numpy as jnp
from jax import lax
from jax.experimental import pallas as pl
from jax.experimental.pallas import tpu as pltpu
from jax.sharding import PartitionSpec as P

LAYERS = 8
C = 192
CP = 256
T = 16
KT = 14 * 128
STRIP = 16
PIECE = 288
SMALL = 16
FIRST = 2


def tap_piece(weight, tile):
    tap = lax.dynamic_index_in_dim(weight, jnp.minimum(tile, 26), 0, keepdims=False).T
    low = tap[:, :128]
    high = jnp.concatenate([tap[: C // 2, 128:], tap[C // 2 :, 128:]], axis=1)
    return jnp.concatenate([low, high], axis=0)


def three_parts(vector):
    high = lax.reduce_precision(vector, 8, 7)
    rest = vector - high
    middle = lax.reduce_precision(rest, 8, 7)
    return jnp.stack([high, middle, rest - middle]).astype(jnp.bfloat16)


def layer_kernel(
    win, base_ref, top_ref, r0_ref, r1_ref, r2_ref, bot_ref, w_ref, gain_ref, bias_ref,
    o0_ref, o1_ref, o2_ref, x9, wbuf,
):
    wout = win - 2
    for b in range(3):
        for e in range(3):
            for a in range(3):
                tap = 9 * a + 3 * b + e
                for lo, hi, src in ((0, 96, 0), (96, 192, 1)):
                    rows = w_ref[tap, lo:hi, :]
                    high = w_ref[tap, 192:288, :].astype(jnp.float32)
                    if src:
                        high = pltpu.roll(high, 64, 1)
                    lane = lax.broadcasted_iota(jnp.int32, high.shape, 1)
                    high = jnp.where(lane < 64, high, 0.0).astype(jnp.bfloat16)
                    both = jnp.concatenate([rows, high], axis=1)
                    full = (e * 3 + a) * 128
                    if a < 2:
                        half = (9 + e) * 128 + 64 * a
                    else:
                        half = 12 * 128 + 64 * e
                    if src == 0:
                        wbuf[b, full : full + 96, :] = both
                    else:
                        wbuf[b, full + 96 : full + 128, :] = both[:32]
                        wbuf[b, half : half + 64, :] = both[32:]
        wbuf[b, KT - 64 : KT, :] = jnp.zeros((64, CP), jnp.bfloat16)

    gain = gain_ref[...].reshape(1, 1, CP)
    for row, ref in enumerate((top_ref, r0_ref, r1_ref, r2_ref, bot_ref)):

        @pl.loop(0, win, step=2)
        def _(col, row=row, ref=ref):
            v = ref[pl.ds(col, 2)].astype(jnp.float32)
            ms = jnp.sum(v * v, axis=2, keepdims=True) * (1.0 / C)
            g = v * lax.rsqrt(ms + 1e-6) * gain
            h = g / (1.0 + jnp.exp(-g))
            time = lax.broadcasted_iota(jnp.int32, h.shape, 1)
            late1 = jnp.where(time >= 1, pltpu.roll(h, 1, 1), 0.0)
            late2 = jnp.where(time >= 2, pltpu.roll(h, 2, 1), 0.0)
            by_tap = [late2, late1, h]
            low = [p[:, :, :128].astype(jnp.bfloat16) for p in by_tap]
            pair = (late2[:, :, 128:] + pltpu.roll(late1[:, :, 128:], 64, 2)).astype(
                jnp.bfloat16
            )
            last = h[:, :, 128:].astype(jnp.bfloat16)
            moved = pltpu.roll(h[:, :, 128:], 64, 2).astype(jnp.bfloat16)
            for e in range(3):
                at = pl.ds(col + 2 - e, 2)
                for a in range(3):
                    tile = e * 3 + a
                    x9[row, at, :, tile * 128 : (tile + 1) * 128] = low[a]
                x9[row, at, :, (9 + e) * 128 : (10 + e) * 128] = pair
            x9[row, pl.ds(col + 2, 2), :, 12 * 128 : 13 * 128] = last
            before = x9[row, pl.ds(col + 1, 2), :, 12 * 128 : 13 * 128]
            lane = lax.broadcasted_iota(jnp.int32, before.shape, 2)
            x9[row, pl.ds(col + 1, 2), :, 12 * 128 : 13 * 128] = jnp.where(
                lane < 64, before, moved
            )
            x9[row, pl.ds(col, 2), :, 13 * 128 : 14 * 128] = last

    bias = bias_ref[...].reshape(1, 1, CP)
    for row, (src, out) in enumerate(((r0_ref, o0_ref), (r1_ref, o1_ref), (r2_ref, o2_ref))):
        acc = jnp.zeros((wout * T, CP), jnp.float32)
        for b in range(3):
            left = x9[row + b, 2 : 2 + wout].reshape(wout * T, KT)
            acc = acc + jnp.dot(left, wbuf[b], preferred_element_type=jnp.float32)
        new = src[1 : 1 + wout].astype(jnp.float32) + acc.reshape(wout, T, CP) + bias
        where = base_ref[0] + 1 + lax.broadcasted_iota(jnp.int32, new.shape, 0)
        inside = jnp.logical_and(where >= 0, where < 128)
        out[...] = jnp.where(inside, new, 0.0).astype(jnp.bfloat16)


def run_layer(win, which, base, top, rows, bot, weights, gain, bias):
    wout = win - 2
    whole = pl.BlockSpec(memory_space=pltpu.VMEM)
    row_shape = jax.ShapeDtypeStruct((wout, T, CP), jnp.bfloat16)
    return pl.pallas_call(
        functools.partial(layer_kernel, win),
        grid=(1,),
        out_shape=[row_shape] * 3,
        in_specs=[pl.BlockSpec(memory_space=pltpu.SMEM)]
        + [pl.BlockSpec((win, T, CP), lambda i: (0, 0, 0))] * 5
        + [pl.BlockSpec((32, None, PIECE, 128), lambda i: (0, which, 0, 0))]
        + [pl.BlockSpec((1, CP), lambda i: (0, 0))] * 2,
        out_specs=[pl.BlockSpec((wout, T, CP), lambda i: (0, 0, 0))] * 3,
        scratch_shapes=[
            pltpu.VMEM((5, win + 2, T, KT), jnp.bfloat16),
            pltpu.VMEM((3, KT, CP), jnp.bfloat16),
        ],
        compiler_params=pltpu.CompilerParams(vmem_limit_bytes=40 * 1024 * 1024),
        cost_estimate=pl.CostEstimate(
            flops=2 * 3 * wout * T * 9 * 3 * C * C, bytes_accessed=4 << 20, transcendentals=0
        ),
    )(base, top, *rows, bot, weights, gain, bias)


def on_device(frames_in, norm_gain, conv_weight, conv_bias):
    section = lax.axis_index("section")
    tile = lax.axis_index("tile")
    tiles = lax.axis_size("tile")

    small = jnp.concatenate(
        [three_parts(norm_gain[0]).reshape(-1), three_parts(conv_bias[0]).reshape(-1)]
    )
    small = jnp.pad(small, (0, SMALL * 128 - small.shape[0])).reshape(SMALL, 128)
    piece = jnp.concatenate([tap_piece(conv_weight[0], tile), small], axis=0)
    rel = [piece]
    for k in range(1, LAYERS):
        rel.append(
            lax.ppermute(piece, "section", [(i, (i + k) % LAYERS) for i in range(LAYERS)])
        )
    rel = jnp.stack(rel)
    order = jnp.mod(section - jnp.arange(LAYERS), LAYERS)
    pieces = jnp.take(rel, order, axis=0)
    parts = (
        pieces[:, PIECE:].astype(jnp.float32).reshape(LAYERS, SMALL * 128)[:, : 6 * C]
    ).reshape(LAYERS, 2, 3, C)
    vectors = parts[:, :, 0] + parts[:, :, 1] + parts[:, :, 2]
    vectors = jnp.pad(vectors, ((0, 0), (0, 0), (0, CP - C)))
    early = lax.all_gather(pieces[:FIRST, :PIECE], "tile")
    late = lax.all_gather(pieces[FIRST:, :PIECE], "tile")

    padded = jnp.pad(frames_in, ((0, 0), (0, 0), (0, 0), (LAYERS, LAYERS)))
    strip = lax.dynamic_slice_in_dim(padded, section * STRIP, STRIP + 2 * LAYERS, axis=3)
    strip = jnp.pad(strip.transpose(2, 3, 0, 1), ((0, 0), (0, 0), (0, 0), (0, CP - C)))
    rows = [strip[0], strip[1], strip[2]]
    down = [(i, i + 1) for i in range(tiles - 1)]
    up = [(i + 1, i) for i in range(tiles - 1)]
    for layer in range(LAYERS):
        win = STRIP + 2 * (LAYERS - layer)
        top = lax.ppermute(rows[2], "tile", down)
        bot = lax.ppermute(rows[0], "tile", up)
        base = (section * STRIP - (LAYERS - layer)).astype(jnp.int32).reshape(1)
        weights, which = (early, layer) if layer < FIRST else (late, layer - FIRST)
        rows = run_layer(
            win, which, base, top, rows, bot, weights,
            vectors[layer, 0:1], vectors[layer, 1:2],
        )

    share = T // LAYERS
    out = jnp.stack([row[:, :, :C] for row in rows])
    out = out.transpose(2, 0, 1, 3).reshape(LAYERS, share, 3, STRIP, C)
    out = lax.all_to_all(out, "section", 0, 0, tiled=True)
    return out.transpose(1, 4, 2, 0, 3).reshape(share, C, 3, LAYERS * STRIP)


def solution(mesh):
    placed = (
        P(None, None, "tile", None),
        P("section", None),
        P("section", None, None, None),
        P("section", None),
    )
    return jax.shard_map(
        on_device,
        mesh=mesh,
        in_specs=placed,
        out_specs=P("section", None, "tile", None),
        check_vma=False,
    )
```

```python
import functools

import jax
import jax.numpy as jnp
from jax import lax
from jax.experimental import pallas as pl
from jax.experimental.pallas import tpu as pltpu
from jax.sharding import PartitionSpec as P

LAYERS = 8
C = 192
CP = 256
T = 16
KT = 14 * 128
STRIP = 16
PIECE = 288
SMALL = 16
FIRST = 2
CH = 4


def tap_piece(weight, tile):
    tap = lax.dynamic_index_in_dim(weight, jnp.minimum(tile, 26), 0, keepdims=False).T
    low = tap[:, :128]
    high = jnp.concatenate([tap[: C // 2, 128:], tap[C // 2 :, 128:]], axis=1)
    return jnp.concatenate([low, high], axis=0)


def three_parts(vector):
    high = lax.reduce_precision(vector, 8, 7)
    rest = vector - high
    middle = lax.reduce_precision(rest, 8, 7)
    return jnp.stack([high, middle, rest - middle]).astype(jnp.bfloat16)


def unpack(flip, w_ref, wbuf):
    lane = lax.broadcasted_iota(jnp.int32, (C // 2, 128), 1)
    for b in range(3):
        b_at = b + flip * (2 - 2 * b)
        for e in range(3):
            full = (b * 3 + e) * 128
            half = (9 + e) * 128 + 64 * (b - 1) if b else 12 * 128 + 64 * e
            for a in range(3):
                tap = 9 * a + 3 * b_at + e
                high = w_ref[tap, C : C + C // 2, :].astype(jnp.float32)
                one = jnp.where(lane < 64, high, 0.0).astype(jnp.bfloat16)
                two = jnp.where(lane < 64, pltpu.roll(high, 64, 1), 0.0).astype(jnp.bfloat16)
                at = a * CP
                wbuf[full : full + 128, at : at + 128] = w_ref[tap, 0:128, :]
                wbuf[half : half + 64, at : at + 128] = w_ref[tap, 128:C, :]
                wbuf[full : full + 96, at + 128 : at + CP] = one
                wbuf[full + 96 : full + 128, at + 128 : at + CP] = two[:32]
                wbuf[half : half + 64, at + 128 : at + CP] = two[32:]
    wbuf[KT - 64 : KT, :] = jnp.zeros((64, 3 * CP), jnp.bfloat16)


def normed(v, half_gain):
    v = v.astype(jnp.float32)
    ms = jnp.sum(v * v, axis=2, keepdims=True) * (1.0 / C)
    u = v * lax.rsqrt(ms + 1e-6) * half_gain
    return u + u * jnp.tanh(u)


def place_lone(buf, col, tile, value, moved):
    step = value.shape[0]
    buf[pl.ds(col + 2, step), :, tile * 128 : (tile + 1) * 128] = value
    before = buf[pl.ds(col + 1, step), :, tile * 128 : (tile + 1) * 128]
    lane = lax.broadcasted_iota(jnp.int32, before.shape, 2)
    buf[pl.ds(col + 1, step), :, tile * 128 : (tile + 1) * 128] = jnp.where(
        lane < 64, before, moved
    )
    buf[pl.ds(col, step), :, (tile + 1) * 128 : (tile + 2) * 128] = value


def time_summed(start, left, w_ref, lo, hi):
    wout = start.shape[0]
    time = lax.broadcasted_iota(jnp.int32, start.shape, 1)
    for a in range(3):
        part = jnp.dot(
            left, w_ref[lo:hi, a * CP : (a + 1) * CP], preferred_element_type=jnp.float32
        ).reshape(wout, T, CP)
        if a < 2:
            part = jnp.where(time >= 2 - a, pltpu.roll(part, 2 - a, 1), 0.0)
        start = start + part
    return start


def in_frame(value, first):
    where = first + lax.broadcasted_iota(jnp.int32, value.shape, 0)
    inside = jnp.logical_and(where >= 0, where < 128)
    return jnp.where(inside, value, 0.0).astype(jnp.bfloat16)


def inner_kernel(
    win, place_ref, r0_ref, r1_ref, r2_ref, in_ref, w_ref, gain_ref, bias_ref,
    acc_ref, n1_ref, n2_ref, outer_ref, x9, wbuf,
):
    wout = win - 2
    unpack(place_ref[1], w_ref, wbuf)
    outer_ref[0:384, :] = wbuf[0:384, :]
    outer_ref[384:640, :] = wbuf[12 * 128 : 14 * 128, :]
    gain = (0.5 * gain_ref[...]).reshape(1, 1, CP)

    for col in range(0, win, CH):
        step = min(CH, win - col)
        low, high, moved = [None], [None], [None]
        for ref in (r0_ref, r1_ref, r2_ref, in_ref):
            h = normed(ref[pl.ds(col, step)], gain)
            low.append(h[:, :, :128].astype(jnp.bfloat16))
            high.append(h[:, :, 128:])
            moved.append(pltpu.roll(h[:, :, 128:], 64, 2))
        for r in range(3):
            pair = (high[r + 1] + moved[r + 2]).astype(jnp.bfloat16)
            for e in range(3):
                at = pl.ds(col + 2 - e, step)
                for b in range(0 if r else 1, 3):
                    tile = b * 3 + e
                    x9[r, at, :, tile * 128 : (tile + 1) * 128] = low[r + b]
                x9[r, at, :, (9 + e) * 128 : (10 + e) * 128] = pair
            if r:
                place_lone(
                    x9.at[r], col, 12, high[r].astype(jnp.bfloat16), moved[r].astype(jnp.bfloat16)
                )

    bias = bias_ref[...].reshape(1, 1, CP)
    first = place_ref[0] + 1
    for row, src, out in ((0, r0_ref, acc_ref), (2, r2_ref, n2_ref), (1, r1_ref, n1_ref)):
        lo, hi = (0, KT) if row else (3 * 128, 12 * 128)
        left = x9[row, 2 : 2 + wout, :, lo:hi].reshape(wout * T, hi - lo)
        new = time_summed(src[1 : 1 + wout].astype(jnp.float32) + bias, left, wbuf, lo, hi)
        out[...] = in_frame(new, first) if row else new


def outer_kernel(win, place_ref, out_ref, acc_ref, w_ref, gain_ref, n0_ref, x5):
    wout = win - 2
    gain = (0.5 * gain_ref[...]).reshape(1, 1, CP)

    for col in range(0, win, CH):
        step = min(CH, win - col)
        h = normed(out_ref[pl.ds(col, step)], gain)
        low = h[:, :, :128].astype(jnp.bfloat16)
        high = h[:, :, 128:]
        for e in range(3):
            x5[pl.ds(col + 2 - e, step), :, e * 128 : (e + 1) * 128] = low
        place_lone(
            x5, col, 3, high.astype(jnp.bfloat16), pltpu.roll(high, 64, 2).astype(jnp.bfloat16)
        )

    left = x5[2 : 2 + wout].reshape(wout * T, 640)
    n0_ref[...] = in_frame(time_summed(acc_ref[...], left, w_ref, 0, 640), place_ref[0] + 1)


def run_inner(win, which, place, rows, inner, weights, gain, bias):
    wout = win - 2
    row_in = pl.BlockSpec((win, T, CP), lambda i: (0, 0, 0))
    row_out = pl.BlockSpec((wout, T, CP), lambda i: (0, 0, 0))
    vector = pl.BlockSpec((1, CP), lambda i: (0, 0))
    return pl.pallas_call(
        functools.partial(inner_kernel, win),
        grid=(1,),
        out_shape=[
            jax.ShapeDtypeStruct((wout, T, CP), jnp.float32),
            jax.ShapeDtypeStruct((wout, T, CP), jnp.bfloat16),
            jax.ShapeDtypeStruct((wout, T, CP), jnp.bfloat16),
            jax.ShapeDtypeStruct((640, 3 * CP), jnp.bfloat16),
        ],
        in_specs=[pl.BlockSpec(memory_space=pltpu.SMEM)]
        + [row_in] * 4
        + [pl.BlockSpec((32, None, PIECE, 128), lambda i: (0, which, 0, 0))]
        + [vector] * 2,
        out_specs=[row_out] * 3 + [pl.BlockSpec((640, 3 * CP), lambda i: (0, 0))],
        scratch_shapes=[
            pltpu.VMEM((3, win + 2, T, KT), jnp.bfloat16),
            pltpu.VMEM((KT, 3 * CP), jnp.bfloat16),
        ],
        compiler_params=pltpu.CompilerParams(vmem_limit_bytes=40 * 1024 * 1024),
        cost_estimate=pl.CostEstimate(
            flops=4 * 3 * wout * T * 9 * 3 * C * C, bytes_accessed=4 << 20, transcendentals=0
        ),
    )(place, *rows, inner, weights, gain, bias)


def run_outer(win, place, outer, acc, weights, gain):
    wout = win - 2
    return pl.pallas_call(
        functools.partial(outer_kernel, win),
        grid=(1,),
        out_shape=jax.ShapeDtypeStruct((wout, T, CP), jnp.bfloat16),
        in_specs=[
            pl.BlockSpec(memory_space=pltpu.SMEM),
            pl.BlockSpec((win, T, CP), lambda i: (0, 0, 0)),
            pl.BlockSpec((wout, T, CP), lambda i: (0, 0, 0)),
            pl.BlockSpec((640, 3 * CP), lambda i: (0, 0)),
            pl.BlockSpec((1, CP), lambda i: (0, 0)),
        ],
        out_specs=pl.BlockSpec((wout, T, CP), lambda i: (0, 0, 0)),
        scratch_shapes=[pltpu.VMEM((win + 2, T, 640), jnp.bfloat16)],
        compiler_params=pltpu.CompilerParams(vmem_limit_bytes=24 * 1024 * 1024),
        cost_estimate=pl.CostEstimate(
            flops=2 * wout * T * 9 * C * C, bytes_accessed=2 << 20, transcendentals=0
        ),
    )(place, outer, acc, weights, gain)


def on_device(frames_in, norm_gain, conv_weight, conv_bias):
    section = lax.axis_index("section")
    tile = lax.axis_index("tile")
    tiles = lax.axis_size("tile")
    flip = tile % 2
    inner_pairs = [(i, i ^ 1) for i in range(tiles)]
    outer_pairs = [(i, i + 1) for i in range(1, tiles - 1, 2)]
    outer_pairs += [(i + 1, i) for i, _ in outer_pairs]
    same_core = [[i + c for i in range(0, tiles, 2)] for c in range(2)]

    padded = jnp.pad(frames_in, ((0, 0), (0, 0), (0, 0), (LAYERS, LAYERS)))
    strip = lax.dynamic_slice_in_dim(padded, section * STRIP, STRIP + 2 * LAYERS, axis=3)
    strip = jnp.pad(strip.transpose(2, 3, 0, 1), ((0, 0), (0, 0), (0, 0), (0, CP - C)))
    rows = [
        jnp.where(flip == 1, strip[2], strip[0]),
        strip[1],
        jnp.where(flip == 1, strip[0], strip[2]),
    ]

    small = jnp.concatenate(
        [three_parts(norm_gain[0]).reshape(-1), three_parts(conv_bias[0]).reshape(-1)]
    )
    small = jnp.pad(small, (0, SMALL * 128 - small.shape[0])).reshape(SMALL, 128)
    piece = jnp.concatenate([tap_piece(conv_weight[0], tile), small], axis=0)
    pieces = lax.all_to_all(
        jnp.broadcast_to(piece[None], (LAYERS,) + piece.shape), "section", 0, 0, tiled=True
    )
    parts = (
        pieces[:, PIECE:].astype(jnp.float32).reshape(LAYERS, SMALL * 128)[:, : 6 * C]
    ).reshape(LAYERS, 2, 3, C)
    vectors = parts[:, :, 0] + parts[:, :, 1] + parts[:, :, 2]
    vectors = jnp.pad(vectors, ((0, 0), (0, 0), (0, CP - C)))
    late = lax.all_gather(pieces[FIRST:, :PIECE], "tile")
    first = jnp.broadcast_to(pieces[None, :FIRST, :PIECE], (tiles // 2, FIRST, PIECE, 128))
    mine = lax.all_to_all(first, "tile", 0, 0, axis_index_groups=same_core, tiled=True)
    theirs = lax.ppermute(mine, "tile", inner_pairs)
    even = jnp.where(flip == 0, mine, theirs)
    odd = jnp.where(flip == 0, theirs, mine)
    early = jnp.stack([even, odd], axis=1).reshape(tiles, FIRST, PIECE, 128)

    inner = lax.ppermute(rows[2], "tile", inner_pairs)
    for layer in range(LAYERS):
        win = STRIP + 2 * (LAYERS - layer)
        outer = lax.ppermute(rows[0], "tile", outer_pairs)
        place = jnp.stack([section * STRIP - (LAYERS - layer), flip]).astype(jnp.int32)
        weights, which = (early, layer) if layer < FIRST else (late, layer - FIRST)
        gain, bias = vectors[layer, 0:1], vectors[layer, 1:2]
        acc, row1, row2, w_outer = run_inner(
            win, which, place, rows, inner, weights, gain, bias
        )
        if layer + 1 < LAYERS:
            inner = lax.ppermute(row2, "tile", inner_pairs)
        row0 = run_outer(win, place, outer, acc, w_outer, gain)
        rows = [row0, row1, row2]

    share = T // LAYERS
    upper = jnp.where(flip == 1, rows[2], rows[0])
    lower = jnp.where(flip == 1, rows[0], rows[2])
    out = jnp.stack([row[:, :, :C] for row in (upper, rows[1], lower)])
    out = out.transpose(2, 0, 1, 3).reshape(LAYERS, share, 3, STRIP, C)
    out = lax.all_to_all(out, "section", 0, 0, tiled=True)
    return out.transpose(1, 4, 2, 0, 3).reshape(share, C, 3, LAYERS * STRIP)


def solution(mesh):
    placed = (
        P(None, None, "tile", None),
        P("section", None),
        P("section", None, None, None),
        P("section", None),
    )
    return jax.shard_map(
        on_device,
        mesh=mesh,
        in_specs=placed,
        out_specs=P("section", None, "tile", None),
        check_vma=False,
    )
```

```python
import functools

import jax
import jax.numpy as jnp
from jax import lax
from jax.experimental import pallas as pl
from jax.experimental.pallas import tpu as pltpu
from jax.sharding import PartitionSpec as P

LAYERS = 8
C = 192
CP = 256
T = 16
KT = 14 * 128
STRIP = 16
PIECE = 288
SMALL = 16
FIRST = 2
CH = 4


def tap_piece(weight, tile):
    tap = lax.dynamic_index_in_dim(weight, jnp.minimum(tile, 26), 0, keepdims=False).T
    low = tap[:, :128]
    high = jnp.concatenate([tap[: C // 2, 128:], tap[C // 2 :, 128:]], axis=1)
    return jnp.concatenate([low, high], axis=0)


def three_parts(vector):
    high = lax.reduce_precision(vector, 8, 7)
    rest = vector - high
    middle = lax.reduce_precision(rest, 8, 7)
    return jnp.stack([high, middle, rest - middle]).astype(jnp.bfloat16)


def unpack(flip, w_refs, wbuf):
    def piece(tap, rows):
        if len(w_refs) == 1:
            return w_refs[0][tap, rows, :]
        mine = lax.rem(tap, 2) == flip
        pick = [ref[lax.div(tap, 2), rows, :] for ref in w_refs]
        return jnp.where(mine, pick[0], pick[1])

    lane = lax.broadcasted_iota(jnp.int32, (C // 2, 128), 1)
    for b in range(3):
        b_at = b + flip * (2 - 2 * b)
        for e in range(3):
            full = (b * 3 + e) * 128
            half = (9 + e) * 128 + 64 * (b - 1) if b else 12 * 128 + 64 * e
            for a in range(3):
                tap = 9 * a + 3 * b_at + e
                high = piece(tap, slice(C, C + C // 2)).astype(jnp.float32)
                one = jnp.where(lane < 64, high, 0.0).astype(jnp.bfloat16)
                two = jnp.where(lane < 64, pltpu.roll(high, 64, 1), 0.0).astype(jnp.bfloat16)
                at = a * CP
                wbuf[full : full + 128, at : at + 128] = piece(tap, slice(0, 128))
                wbuf[half : half + 64, at : at + 128] = piece(tap, slice(128, C))
                wbuf[full : full + 96, at + 128 : at + CP] = one
                wbuf[full + 96 : full + 128, at + 128 : at + CP] = two[:32]
                wbuf[half : half + 64, at + 128 : at + CP] = two[32:]
    wbuf[KT - 64 : KT, :] = jnp.zeros((64, 3 * CP), jnp.bfloat16)


def normed(v, half_gain):
    v = v.astype(jnp.float32)
    ms = jnp.sum(v * v, axis=2, keepdims=True) * (1.0 / C)
    u = v * lax.rsqrt(ms + 1e-6) * half_gain
    return u + u * jnp.tanh(u)


def place_lone(buf, col, tile, value, moved):
    step = value.shape[0]
    buf[pl.ds(col + 2, step), :, tile * 128 : (tile + 1) * 128] = value
    before = buf[pl.ds(col + 1, step), :, tile * 128 : (tile + 1) * 128]
    lane = lax.broadcasted_iota(jnp.int32, before.shape, 2)
    buf[pl.ds(col + 1, step), :, tile * 128 : (tile + 1) * 128] = jnp.where(
        lane < 64, before, moved
    )
    buf[pl.ds(col, step), :, (tile + 1) * 128 : (tile + 2) * 128] = value


def time_summed(start, left, w_ref, lo, hi):
    wout = start.shape[0]
    time = lax.broadcasted_iota(jnp.int32, start.shape, 1)
    for a in range(3):
        part = jnp.dot(
            left, w_ref[lo:hi, a * CP : (a + 1) * CP], preferred_element_type=jnp.float32
        ).reshape(wout, T, CP)
        if a < 2:
            part = jnp.where(time >= 2 - a, pltpu.roll(part, 2 - a, 1), 0.0)
        start = start + part
    return start


def in_frame(value, first):
    where = first + lax.broadcasted_iota(jnp.int32, value.shape, 0)
    inside = jnp.logical_and(where >= 0, where < 128)
    return jnp.where(inside, value, 0.0).astype(jnp.bfloat16)


def inner_kernel(
    win, pieces, r0_ref, r1_ref, r2_ref, in_ref, gain_ref, bias_ref, *refs
):
    w_refs, (acc_ref, n1_ref, n2_ref, outer_ref, x9, wbuf) = refs[:pieces], refs[pieces:]
    wout = win - 2
    unpack(lax.axis_index("tile") % 2, w_refs, wbuf)
    outer_ref[0:384, :] = wbuf[0:384, :]
    outer_ref[384:640, :] = wbuf[12 * 128 : 14 * 128, :]
    gain = (0.5 * gain_ref[...]).reshape(1, 1, CP)

    for col in range(0, win, CH):
        step = min(CH, win - col)
        low, high, moved = [None], [None], [None]
        for ref in (r0_ref, r1_ref, r2_ref, in_ref):
            h = normed(ref[pl.ds(col, step)], gain)
            low.append(h[:, :, :128].astype(jnp.bfloat16))
            high.append(h[:, :, 128:])
            moved.append(pltpu.roll(h[:, :, 128:], 64, 2))
        for r in range(3):
            pair = (high[r + 1] + moved[r + 2]).astype(jnp.bfloat16)
            for e in range(3):
                at = pl.ds(col + 2 - e, step)
                for b in range(0 if r else 1, 3):
                    tile = b * 3 + e
                    x9[r, at, :, tile * 128 : (tile + 1) * 128] = low[r + b]
                x9[r, at, :, (9 + e) * 128 : (10 + e) * 128] = pair
            if r:
                place_lone(
                    x9.at[r], col, 12, high[r].astype(jnp.bfloat16), moved[r].astype(jnp.bfloat16)
                )

    bias = bias_ref[...].reshape(1, 1, CP)
    first = lax.axis_index("section") * STRIP + (STRIP - wout) // 2
    for row, src, out in ((0, r0_ref, acc_ref), (2, r2_ref, n2_ref), (1, r1_ref, n1_ref)):
        lo, hi = (0, KT) if row else (3 * 128, 12 * 128)
        left = x9[row, 2 : 2 + wout, :, lo:hi].reshape(wout * T, hi - lo)
        new = time_summed(src[1 : 1 + wout].astype(jnp.float32) + bias, left, wbuf, lo, hi)
        out[...] = in_frame(new, first) if row else new


def outer_kernel(win, out_ref, acc_ref, w_ref, gain_ref, n0_ref, x5):
    wout = win - 2
    gain = (0.5 * gain_ref[...]).reshape(1, 1, CP)

    for col in range(0, win, CH):
        step = min(CH, win - col)
        h = normed(out_ref[pl.ds(col, step)], gain)
        low = h[:, :, :128].astype(jnp.bfloat16)
        high = h[:, :, 128:]
        for e in range(3):
            x5[pl.ds(col + 2 - e, step), :, e * 128 : (e + 1) * 128] = low
        place_lone(
            x5, col, 3, high.astype(jnp.bfloat16), pltpu.roll(high, 64, 2).astype(jnp.bfloat16)
        )

    left = x5[2 : 2 + wout].reshape(wout * T, 640)
    first = lax.axis_index("section") * STRIP + (STRIP - wout) // 2
    n0_ref[...] = in_frame(time_summed(acc_ref[...], left, w_ref, 0, 640), first)


def run_inner(win, which, rows, inner, weights, gain, bias):
    wout = win - 2
    row_in = pl.BlockSpec((win, T, CP), lambda i: (0, 0, 0))
    row_out = pl.BlockSpec((wout, T, CP), lambda i: (0, 0, 0))
    vector = pl.BlockSpec((1, CP), lambda i: (0, 0))
    return pl.pallas_call(
        functools.partial(inner_kernel, win, len(weights)),
        grid=(1,),
        out_shape=[
            pltpu.VMEM((wout, T, CP), jnp.float32),
            jax.ShapeDtypeStruct((wout, T, CP), jnp.bfloat16),
            jax.ShapeDtypeStruct((wout, T, CP), jnp.bfloat16),
            pltpu.VMEM((640, 3 * CP), jnp.bfloat16),
        ],
        in_specs=[row_in] * 4
        + [vector] * 2
        + [
            pl.BlockSpec((w.shape[0], None, PIECE, 128), lambda i: (0, which, 0, 0))
            for w in weights
        ],
        out_specs=[row_out] * 3 + [pl.BlockSpec((640, 3 * CP), lambda i: (0, 0))],
        scratch_shapes=[
            pltpu.VMEM((3, win + 2, T, KT), jnp.bfloat16),
            pltpu.VMEM((KT, 3 * CP), jnp.bfloat16),
        ],
        compiler_params=pltpu.CompilerParams(vmem_limit_bytes=40 * 1024 * 1024),
        cost_estimate=pl.CostEstimate(
            flops=4 * 3 * wout * T * 9 * 3 * C * C, bytes_accessed=4 << 20, transcendentals=0
        ),
    )(*rows, inner, gain, bias, *weights)


def run_outer(win, outer, acc, weights, gain):
    wout = win - 2
    return pl.pallas_call(
        functools.partial(outer_kernel, win),
        grid=(1,),
        out_shape=jax.ShapeDtypeStruct((wout, T, CP), jnp.bfloat16),
        in_specs=[
            pl.BlockSpec((win, T, CP), lambda i: (0, 0, 0)),
            pl.BlockSpec((wout, T, CP), lambda i: (0, 0, 0)),
            pl.BlockSpec((640, 3 * CP), lambda i: (0, 0)),
            pl.BlockSpec((1, CP), lambda i: (0, 0)),
        ],
        out_specs=pl.BlockSpec((wout, T, CP), lambda i: (0, 0, 0)),
        scratch_shapes=[pltpu.VMEM((win + 2, T, 640), jnp.bfloat16)],
        compiler_params=pltpu.CompilerParams(vmem_limit_bytes=24 * 1024 * 1024),
        cost_estimate=pl.CostEstimate(
            flops=2 * wout * T * 9 * C * C, bytes_accessed=2 << 20, transcendentals=0
        ),
    )(outer, acc, weights, gain)


def on_device(frames_in, norm_gain, conv_weight, conv_bias):
    section = lax.axis_index("section")
    tile = lax.axis_index("tile")
    tiles = lax.axis_size("tile")
    flip = tile % 2
    inner_pairs = [(i, i ^ 1) for i in range(tiles)]
    outer_pairs = [(i, i + 1) for i in range(1, tiles - 1, 2)]
    outer_pairs += [(i + 1, i) for i, _ in outer_pairs]
    same_core = [[i + c for i in range(0, tiles, 2)] for c in range(2)]

    padded = jnp.pad(frames_in, ((0, 0), (0, 0), (0, 0), (LAYERS, LAYERS)))
    strip = lax.dynamic_slice_in_dim(padded, section * STRIP, STRIP + 2 * LAYERS, axis=3)
    strip = jnp.pad(strip.transpose(2, 3, 0, 1), ((0, 0), (0, 0), (0, 0), (0, CP - C)))
    rows = [
        jnp.where(flip == 1, strip[2], strip[0]),
        strip[1],
        jnp.where(flip == 1, strip[0], strip[2]),
    ]

    small = jnp.concatenate(
        [three_parts(norm_gain[0]).reshape(-1), three_parts(conv_bias[0]).reshape(-1)]
    )
    small = jnp.pad(small, (0, SMALL * 128 - small.shape[0])).reshape(SMALL, 128)
    piece = jnp.concatenate([tap_piece(conv_weight[0], tile), small], axis=0)
    pieces = lax.all_to_all(
        jnp.broadcast_to(piece[None], (LAYERS,) + piece.shape), "section", 0, 0, tiled=True
    )
    parts = (
        pieces[:, PIECE:].astype(jnp.float32).reshape(LAYERS, SMALL * 128)[:, : 6 * C]
    ).reshape(LAYERS, 2, 3, C)
    vectors = parts[:, :, 0] + parts[:, :, 1] + parts[:, :, 2]
    vectors = jnp.pad(vectors, ((0, 0), (0, 0), (0, CP - C)))
    late = (lax.all_gather(pieces[FIRST:, :PIECE], "tile"),)
    first = jnp.broadcast_to(pieces[None, :FIRST, :PIECE], (tiles // 2, FIRST, PIECE, 128))
    mine = lax.all_to_all(first, "tile", 0, 0, axis_index_groups=same_core, tiled=True)
    theirs = lax.ppermute(mine, "tile", inner_pairs)
    early = (mine, theirs)

    inner = lax.ppermute(rows[2], "tile", inner_pairs)
    for layer in range(LAYERS):
        win = STRIP + 2 * (LAYERS - layer)
        outer = lax.ppermute(rows[0], "tile", outer_pairs)
        weights, which = (early, layer) if layer < FIRST else (late, layer - FIRST)
        gain, bias = vectors[layer, 0:1], vectors[layer, 1:2]
        acc, row1, row2, w_outer = run_inner(win, which, rows, inner, weights, gain, bias)
        if layer + 1 < LAYERS:
            inner = lax.ppermute(row2, "tile", inner_pairs)
        row0 = run_outer(win, outer, acc, w_outer, gain)
        rows = [row0, row1, row2]

    share = T // LAYERS
    upper = jnp.where(flip == 1, rows[2], rows[0])
    lower = jnp.where(flip == 1, rows[0], rows[2])
    out = jnp.stack([row[:, :, :C] for row in (upper, rows[1], lower)])
    out = out.transpose(2, 0, 1, 3).reshape(LAYERS, share, 3, STRIP, C)
    out = lax.all_to_all(out, "section", 0, 0, tiled=True)
    return out.transpose(1, 4, 2, 0, 3).reshape(share, C, 3, LAYERS * STRIP)


def solution(mesh):
    placed = (
        P(None, None, "tile", None),
        P("section", None),
        P("section", None, None, None),
        P("section", None),
    )
    return jax.shard_map(
        on_device,
        mesh=mesh,
        in_specs=placed,
        out_specs=P("section", None, "tile", None),
        check_vma=False,
    )
```

```python
import functools

import jax
import jax.numpy as jnp
from jax import lax
from jax.experimental import pallas as pl
from jax.experimental.pallas import tpu as pltpu
from jax.sharding import PartitionSpec as P

LAYERS = 8
C = 192
CP = 256
T = 16
KT = 14 * 128
STRIP = 16
PIECE = 288
SMALL = 16
FIRST = 2
CH = 4


def tap_piece(weight, tile):
    tap = lax.dynamic_index_in_dim(weight, jnp.minimum(tile, 26), 0, keepdims=False).T
    low = tap[:, :128]
    high = jnp.concatenate([tap[: C // 2, 128:], tap[C // 2 :, 128:]], axis=1)
    return jnp.concatenate([low, high], axis=0)


def three_parts(vector):
    high = lax.reduce_precision(vector, 8, 7)
    rest = vector - high
    middle = lax.reduce_precision(rest, 8, 7)
    return jnp.stack([high, middle, rest - middle]).astype(jnp.bfloat16)


def unpack(flip, w_refs, wbuf):
    def piece(tap, rows):
        if len(w_refs) == 1:
            return w_refs[0][tap, rows, :]
        mine = lax.rem(tap, 2) == flip
        pick = [ref[lax.div(tap, 2), rows, :] for ref in w_refs]
        return jnp.where(mine, pick[0], pick[1])

    lane = lax.broadcasted_iota(jnp.int32, (C // 2, 128), 1)
    for b in range(3):
        b_at = b + flip * (2 - 2 * b)
        for e in range(3):
            full = (b * 3 + e) * 128
            half = (9 + e) * 128 + 64 * (b - 1) if b else 12 * 128 + 64 * e
            for a in range(3):
                tap = 9 * a + 3 * b_at + e
                high = piece(tap, slice(C, C + C // 2)).astype(jnp.float32)
                one = jnp.where(lane < 64, high, 0.0).astype(jnp.bfloat16)
                two = jnp.where(lane < 64, pltpu.roll(high, 64, 1), 0.0).astype(jnp.bfloat16)
                at = a * CP
                wbuf[full : full + 128, at : at + 128] = piece(tap, slice(0, 128))
                wbuf[half : half + 64, at : at + 128] = piece(tap, slice(128, C))
                wbuf[full : full + 96, at + 128 : at + CP] = one
                wbuf[full + 96 : full + 128, at + 128 : at + CP] = two[:32]
                wbuf[half : half + 64, at + 128 : at + CP] = two[32:]
    wbuf[KT - 64 : KT, :] = jnp.zeros((64, 3 * CP), jnp.bfloat16)


def normed(v, half_gain):
    v = v.astype(jnp.float32)
    ms = jnp.sum(v * v, axis=2, keepdims=True) * (1.0 / C)
    u = v * lax.rsqrt(ms + 1e-6) * half_gain
    return u + u * jnp.tanh(u)


def place_lone(buf, col, tile, value, moved):
    step = value.shape[0]
    buf[pl.ds(col + 2, step), :, tile * 128 : (tile + 1) * 128] = value
    before = buf[pl.ds(col + 1, step), :, tile * 128 : (tile + 1) * 128]
    lane = lax.broadcasted_iota(jnp.int32, before.shape, 2)
    buf[pl.ds(col + 1, step), :, tile * 128 : (tile + 1) * 128] = jnp.where(
        lane < 64, before, moved
    )
    buf[pl.ds(col, step), :, (tile + 1) * 128 : (tile + 2) * 128] = value


def time_summed(start, left, w_ref, lo, hi):
    wout = start.shape[0]
    time = lax.broadcasted_iota(jnp.int32, start.shape, 1)
    for a in range(3):
        part = jnp.dot(
            left, w_ref[lo:hi, a * CP : (a + 1) * CP], preferred_element_type=jnp.float32
        ).reshape(wout, T, CP)
        if a < 2:
            part = jnp.where(time >= 2 - a, pltpu.roll(part, 2 - a, 1), 0.0)
        start = start + part
    return start


def in_frame(value, first):
    where = first + lax.broadcasted_iota(jnp.int32, value.shape, 0)
    inside = jnp.logical_and(where >= 0, where < 128)
    return jnp.where(inside, value, 0.0).astype(jnp.bfloat16)


def inner_kernel(
    win, pieces, r0_ref, r1_ref, r2_ref, in_ref, gain_ref, bias_ref, *refs
):
    w_refs, (acc_ref, n1_ref, n2_ref, outer_ref, x9, wbuf) = refs[:pieces], refs[pieces:]
    wout = win - 2
    unpack(lax.axis_index("tile") % 2, w_refs, wbuf)
    outer_ref[0:384, :] = wbuf[0:384, :]
    outer_ref[384:640, :] = wbuf[12 * 128 : 14 * 128, :]
    gain = (0.5 * gain_ref[...]).reshape(1, 1, CP)

    for col in range(0, win, CH):
        step = min(CH, win - col)
        low, high, moved = [None], [None], [None]
        for ref in (r0_ref, r1_ref, r2_ref, in_ref):
            h = normed(ref[pl.ds(col, step)], gain)
            low.append(h[:, :, :128].astype(jnp.bfloat16))
            high.append(h[:, :, 128:])
            moved.append(pltpu.roll(h[:, :, 128:], 64, 2))
        for r in range(3):
            pair = (high[r + 1] + moved[r + 2]).astype(jnp.bfloat16)
            for e in range(3):
                at = pl.ds(col + 2 - e, step)
                for b in range(0 if r else 1, 3):
                    tile = b * 3 + e
                    x9[r, at, :, tile * 128 : (tile + 1) * 128] = low[r + b]
                x9[r, at, :, (9 + e) * 128 : (10 + e) * 128] = pair
            if r:
                place_lone(
                    x9.at[r], col, 12, high[r].astype(jnp.bfloat16), moved[r].astype(jnp.bfloat16)
                )

    bias = bias_ref[...].reshape(1, 1, CP)
    first = lax.axis_index("section") * STRIP + (STRIP - wout) // 2
    for row, src, out in ((1, r1_ref, n1_ref), (0, r0_ref, acc_ref), (2, r2_ref, n2_ref)):
        lo, hi = (0, KT) if row else (3 * 128, 12 * 128)
        left = x9[row, 2 : 2 + wout, :, lo:hi].reshape(wout * T, hi - lo)
        new = time_summed(src[1 : 1 + wout].astype(jnp.float32) + bias, left, wbuf, lo, hi)
        out[...] = in_frame(new, first) if row else new


def outer_kernel(win, out_ref, acc_ref, w_ref, gain_ref, n0_ref, x5):
    wout = win - 2
    gain = (0.5 * gain_ref[...]).reshape(1, 1, CP)

    for col in range(0, win, CH):
        step = min(CH, win - col)
        h = normed(out_ref[pl.ds(col, step)], gain)
        low = h[:, :, :128].astype(jnp.bfloat16)
        high = h[:, :, 128:]
        for e in range(3):
            x5[pl.ds(col + 2 - e, step), :, e * 128 : (e + 1) * 128] = low
        place_lone(
            x5, col, 3, high.astype(jnp.bfloat16), pltpu.roll(high, 64, 2).astype(jnp.bfloat16)
        )

    left = x5[2 : 2 + wout].reshape(wout * T, 640)
    first = lax.axis_index("section") * STRIP + (STRIP - wout) // 2
    n0_ref[...] = in_frame(time_summed(acc_ref[...], left, w_ref, 0, 640), first)


def run_inner(win, which, rows, inner, weights, gain, bias):
    wout = win - 2
    row_in = row_out = vector = pl.BlockSpec(memory_space=pltpu.VMEM)
    return pl.pallas_call(
        functools.partial(inner_kernel, win, len(weights)),
        grid=(1,),
        out_shape=[
            pltpu.VMEM((wout, T, CP), jnp.float32),
            jax.ShapeDtypeStruct((wout, T, CP), jnp.bfloat16),
            jax.ShapeDtypeStruct((wout, T, CP), jnp.bfloat16),
            pltpu.VMEM((640, 3 * CP), jnp.bfloat16),
        ],
        in_specs=[row_in] * 4
        + [vector] * 2
        + [
            pl.BlockSpec((w.shape[0], None, PIECE, 128), lambda i: (0, which, 0, 0))
            for w in weights
        ],
        out_specs=[row_out] * 3 + [row_out],
        scratch_shapes=[
            pltpu.VMEM((3, win + 2, T, KT), jnp.bfloat16),
            pltpu.VMEM((KT, 3 * CP), jnp.bfloat16),
        ],
        compiler_params=pltpu.CompilerParams(vmem_limit_bytes=22 * 1024 * 1024),
        cost_estimate=pl.CostEstimate(
            flops=4 * 3 * wout * T * 9 * 3 * C * C, bytes_accessed=4 << 20, transcendentals=0
        ),
    )(*rows, inner, gain, bias, *weights)


def run_outer(win, outer, acc, weights, gain):
    wout = win - 2
    return pl.pallas_call(
        functools.partial(outer_kernel, win),
        grid=(1,),
        out_shape=jax.ShapeDtypeStruct((wout, T, CP), jnp.bfloat16),
        in_specs=[
            pl.BlockSpec(memory_space=pltpu.VMEM),
            pl.BlockSpec(memory_space=pltpu.VMEM),
            pl.BlockSpec(memory_space=pltpu.VMEM),
            pl.BlockSpec(memory_space=pltpu.VMEM),
        ],
        out_specs=pl.BlockSpec(memory_space=pltpu.VMEM),
        scratch_shapes=[pltpu.VMEM((win + 2, T, 640), jnp.bfloat16)],
        compiler_params=pltpu.CompilerParams(vmem_limit_bytes=12 * 1024 * 1024),
        cost_estimate=pl.CostEstimate(
            flops=2 * wout * T * 9 * C * C, bytes_accessed=2 << 20, transcendentals=0
        ),
    )(outer, acc, weights, gain)


def on_device(frames_in, norm_gain, conv_weight, conv_bias):
    section = lax.axis_index("section")
    tile = lax.axis_index("tile")
    tiles = lax.axis_size("tile")
    flip = tile % 2
    inner_pairs = [(i, i ^ 1) for i in range(tiles)]
    outer_pairs = [(i, i + 1) for i in range(1, tiles - 1, 2)]
    outer_pairs += [(i + 1, i) for i, _ in outer_pairs]
    same_core = [[i + c for i in range(0, tiles, 2)] for c in range(2)]

    padded = jnp.pad(frames_in, ((0, 0), (0, 0), (0, 0), (LAYERS, LAYERS)))
    strip = lax.dynamic_slice_in_dim(padded, section * STRIP, STRIP + 2 * LAYERS, axis=3)
    strip = jnp.pad(strip.transpose(2, 3, 0, 1), ((0, 0), (0, 0), (0, 0), (0, CP - C)))
    rows = [
        jnp.where(flip == 1, strip[2], strip[0]),
        strip[1],
        jnp.where(flip == 1, strip[0], strip[2]),
    ]

    small = jnp.concatenate(
        [three_parts(norm_gain[0]).reshape(-1), three_parts(conv_bias[0]).reshape(-1)]
    )
    small = jnp.pad(small, (0, SMALL * 128 - small.shape[0])).reshape(SMALL, 128)
    piece = jnp.concatenate([tap_piece(conv_weight[0], tile), small], axis=0)
    pieces = lax.all_to_all(
        jnp.broadcast_to(piece[None], (LAYERS,) + piece.shape), "section", 0, 0, tiled=True
    )
    parts = (
        pieces[:, PIECE:].astype(jnp.float32).reshape(LAYERS, SMALL * 128)[:, : 6 * C]
    ).reshape(LAYERS, 2, 3, C)
    vectors = parts[:, :, 0] + parts[:, :, 1] + parts[:, :, 2]
    vectors = jnp.pad(vectors, ((0, 0), (0, 0), (0, CP - C)))
    late = lax.all_gather(pieces[FIRST:-1, :PIECE], "tile")
    first = jnp.broadcast_to(pieces[None, :FIRST, :PIECE], (tiles // 2, FIRST, PIECE, 128))
    mine = lax.all_to_all(first, "tile", 0, 0, axis_index_groups=same_core, tiled=True)
    theirs = lax.ppermute(mine, "tile", inner_pairs)
    early = (mine, theirs)

    inner = lax.ppermute(rows[2], "tile", inner_pairs)
    for layer in range(LAYERS):
        win = STRIP + 2 * (LAYERS - layer)
        which = layer - FIRST
        if layer < FIRST:
            weights, which = early, layer
        elif layer == FIRST:
            final, late, rows[0] = lax.optimization_barrier(
                (pieces[-1:, :PIECE], late, rows[0])
            )
            final = lax.all_gather(final, "tile")
            weights = (late[:, :1],)
        elif layer < LAYERS - 1:
            weights = (late,)
        else:
            weights, which = (final,), 0
        outer = lax.ppermute(rows[0], "tile", outer_pairs)
        gain, bias = vectors[layer, 0:1], vectors[layer, 1:2]
        acc, row1, row2, w_outer = run_inner(win, which, rows, inner, weights, gain, bias)
        if layer + 1 < LAYERS:
            inner = lax.ppermute(row2, "tile", inner_pairs)
        row0 = run_outer(win, outer, acc, w_outer, gain)
        rows = [row0, row1, row2]

    share = T // LAYERS
    upper = jnp.where(flip == 1, rows[2], rows[0])
    lower = jnp.where(flip == 1, rows[0], rows[2])
    out = jnp.stack([row[:, :, :C] for row in (upper, rows[1], lower)])
    out = out.transpose(2, 0, 1, 3).reshape(LAYERS, share, 3, STRIP, C)
    out = lax.all_to_all(out, "section", 0, 0, tiled=True)
    return out.transpose(1, 4, 2, 0, 3).reshape(share, C, 3, LAYERS * STRIP)


def solution(mesh):
    placed = (
        P(None, None, "tile", None),
        P("section", None),
        P("section", None, None, None),
        P("section", None),
    )
    return jax.shard_map(
        on_device,
        mesh=mesh,
        in_specs=placed,
        out_specs=P("section", None, "tile", None),
        check_vma=False,
    )
```

```python
import functools

import jax
import jax.numpy as jnp
from jax import lax
from jax.experimental import pallas as pl
from jax.experimental.pallas import tpu as pltpu
from jax.sharding import PartitionSpec as P

LAYERS = 8
C = 192
CP = 256
T = 16
KT = 14 * 128
STRIP = 16
PIECE = 288
SMALL = 16
FIRST = 2
CH = 4


def tap_piece(weight, tile):
    tap = lax.dynamic_index_in_dim(weight, jnp.minimum(tile, 26), 0, keepdims=False).T
    low = tap[:, :128]
    high = jnp.concatenate([tap[: C // 2, 128:], tap[C // 2 :, 128:]], axis=1)
    return jnp.concatenate([low, high], axis=0)


def three_parts(vector):
    high = lax.reduce_precision(vector, 8, 7)
    rest = vector - high
    middle = lax.reduce_precision(rest, 8, 7)
    return jnp.stack([high, middle, rest - middle]).astype(jnp.bfloat16)


def unpack(flip, w_refs, wbuf):
    def piece(tap, rows):
        if len(w_refs) == 1:
            return w_refs[0][tap, rows, :]
        mine = lax.rem(tap, 2) == flip
        pick = [ref[lax.div(tap, 2), rows, :] for ref in w_refs]
        return jnp.where(mine, pick[0], pick[1])

    lane = lax.broadcasted_iota(jnp.int32, (C // 2, 128), 1)
    for b in range(3):
        b_at = b + flip * (2 - 2 * b)
        for e in range(3):
            full = (b * 3 + e) * 128
            half = (9 + e) * 128 + 64 * (b - 1) if b else 12 * 128 + 64 * e
            for a in range(3):
                tap = 9 * a + 3 * b_at + e
                high = piece(tap, slice(C, C + C // 2)).astype(jnp.float32)
                one = jnp.where(lane < 64, high, 0.0).astype(jnp.bfloat16)
                two = jnp.where(lane < 64, pltpu.roll(high, 64, 1), 0.0).astype(jnp.bfloat16)
                at = a * CP
                wbuf[full : full + 128, at : at + 128] = piece(tap, slice(0, 128))
                wbuf[half : half + 64, at : at + 128] = piece(tap, slice(128, C))
                wbuf[full : full + 96, at + 128 : at + CP] = one
                wbuf[full + 96 : full + 128, at + 128 : at + CP] = two[:32]
                wbuf[half : half + 64, at + 128 : at + CP] = two[32:]
    wbuf[KT - 64 : KT, :] = jnp.zeros((64, 3 * CP), jnp.bfloat16)


def normed(v, half_gain):
    v = v.astype(jnp.float32)
    ms = jnp.sum(v * v, axis=2, keepdims=True) * (1.0 / C)
    u = v * lax.rsqrt(ms + 1e-6) * half_gain
    return u + u * jnp.tanh(u)


def place_lone(buf, col, tile, value, moved):
    step = value.shape[0]
    buf[pl.ds(col + 2, step), :, tile * 128 : (tile + 1) * 128] = value
    before = buf[pl.ds(col + 1, step), :, tile * 128 : (tile + 1) * 128]
    lane = lax.broadcasted_iota(jnp.int32, before.shape, 2)
    buf[pl.ds(col + 1, step), :, tile * 128 : (tile + 1) * 128] = jnp.where(
        lane < 64, before, moved
    )
    buf[pl.ds(col, step), :, (tile + 1) * 128 : (tile + 2) * 128] = value


def time_summed(start, left, w_ref, lo, hi):
    wout = start.shape[0]
    time = lax.broadcasted_iota(jnp.int32, start.shape, 1)
    for a in range(3):
        part = jnp.dot(
            left, w_ref[lo:hi, a * CP : (a + 1) * CP], preferred_element_type=jnp.float32
        ).reshape(wout, T, CP)
        if a < 2:
            part = jnp.where(time >= 2 - a, pltpu.roll(part, 2 - a, 1), 0.0)
        start = start + part
    return start


def in_frame(value, first):
    where = first + lax.broadcasted_iota(jnp.int32, value.shape, 0)
    inside = jnp.logical_and(where >= 0, where < 128)
    return jnp.where(inside, value, 0.0).astype(jnp.bfloat16)


def inner_kernel(
    win, pieces, r0_ref, r1_ref, r2_ref, in_ref, gain_ref, bias_ref, *refs
):
    w_refs, (acc_ref, n1_ref, n2_ref, outer_ref, x9, wbuf) = refs[:pieces], refs[pieces:]
    wout = win - 2
    unpack(lax.axis_index("tile") % 2, w_refs, wbuf)
    outer_ref[0:384, :] = wbuf[0:384, :]
    outer_ref[384:640, :] = wbuf[12 * 128 : 14 * 128, :]
    gain = (0.5 * gain_ref[...]).reshape(1, 1, CP)

    for col in range(0, win, CH):
        step = min(CH, win - col)
        low, high, moved = [None], [None], [None]
        for ref in (r0_ref, r1_ref, r2_ref, in_ref):
            h = normed(ref[pl.ds(col, step)], gain)
            low.append(h[:, :, :128].astype(jnp.bfloat16))
            high.append(h[:, :, 128:])
            moved.append(pltpu.roll(h[:, :, 128:], 64, 2))
        for r in range(3):
            pair = (high[r + 1] + moved[r + 2]).astype(jnp.bfloat16)
            for e in range(3):
                at = pl.ds(col + 2 - e, step)
                for b in range(0 if r else 1, 3):
                    tile = b * 3 + e
                    x9[r, at, :, tile * 128 : (tile + 1) * 128] = low[r + b]
                x9[r, at, :, (9 + e) * 128 : (10 + e) * 128] = pair
            if r:
                place_lone(
                    x9.at[r], col, 12, high[r].astype(jnp.bfloat16), moved[r].astype(jnp.bfloat16)
                )

    bias = bias_ref[...].reshape(1, 1, CP)
    first = lax.axis_index("section") * STRIP + (STRIP - wout) // 2
    for row, src, out in ((1, r1_ref, n1_ref), (0, r0_ref, acc_ref), (2, r2_ref, n2_ref)):
        lo, hi = (0, KT) if row else (3 * 128, 12 * 128)
        left = x9[row, 2 : 2 + wout, :, lo:hi].reshape(wout * T, hi - lo)
        new = time_summed(src[1 : 1 + wout].astype(jnp.float32) + bias, left, wbuf, lo, hi)
        out[...] = in_frame(new, first) if row else new


def outer_kernel(win, out_ref, acc_ref, w_ref, gain_ref, n0_ref, x5):
    wout = win - 2
    gain = (0.5 * gain_ref[...]).reshape(1, 1, CP)

    for col in range(0, win, CH):
        step = min(CH, win - col)
        h = normed(out_ref[pl.ds(col, step)], gain)
        low = h[:, :, :128].astype(jnp.bfloat16)
        high = h[:, :, 128:]
        for e in range(3):
            x5[pl.ds(col + 2 - e, step), :, e * 128 : (e + 1) * 128] = low
        place_lone(
            x5, col, 3, high.astype(jnp.bfloat16), pltpu.roll(high, 64, 2).astype(jnp.bfloat16)
        )

    left = x5[2 : 2 + wout].reshape(wout * T, 640)
    first = lax.axis_index("section") * STRIP + (STRIP - wout) // 2
    n0_ref[...] = in_frame(time_summed(acc_ref[...], left, w_ref, 0, 640), first)


def run_inner(win, which, rows, inner, weights, gain, bias):
    wout = win - 2
    row_in = row_out = vector = pl.BlockSpec(memory_space=pltpu.VMEM)
    return pl.pallas_call(
        functools.partial(inner_kernel, win, len(weights)),
        grid=(1,),
        out_shape=[
            pltpu.VMEM((wout, T, CP), jnp.float32),
            jax.ShapeDtypeStruct((wout, T, CP), jnp.bfloat16),
            jax.ShapeDtypeStruct((wout, T, CP), jnp.bfloat16),
            pltpu.VMEM((640, 3 * CP), jnp.bfloat16),
        ],
        in_specs=[row_in] * 4
        + [vector] * 2
        + [
            pl.BlockSpec((w.shape[0], None, PIECE, 128), lambda i: (0, which, 0, 0))
            for w in weights
        ],
        out_specs=[row_out] * 3 + [row_out],
        scratch_shapes=[
            pltpu.VMEM((3, win + 2, T, KT), jnp.bfloat16),
            pltpu.VMEM((KT, 3 * CP), jnp.bfloat16),
        ],
        compiler_params=pltpu.CompilerParams(vmem_limit_bytes=22 * 1024 * 1024),
        cost_estimate=pl.CostEstimate(
            flops=4 * 3 * wout * T * 9 * 3 * C * C, bytes_accessed=4 << 20, transcendentals=0
        ),
    )(*rows, inner, gain, bias, *weights)


def run_outer(win, outer, acc, weights, gain):
    wout = win - 2
    return pl.pallas_call(
        functools.partial(outer_kernel, win),
        grid=(1,),
        out_shape=jax.ShapeDtypeStruct((wout, T, CP), jnp.bfloat16),
        in_specs=[
            pl.BlockSpec(memory_space=pltpu.VMEM),
            pl.BlockSpec(memory_space=pltpu.VMEM),
            pl.BlockSpec(memory_space=pltpu.VMEM),
            pl.BlockSpec(memory_space=pltpu.VMEM),
        ],
        out_specs=pl.BlockSpec(memory_space=pltpu.VMEM),
        scratch_shapes=[pltpu.VMEM((win + 2, T, 640), jnp.bfloat16)],
        compiler_params=pltpu.CompilerParams(vmem_limit_bytes=12 * 1024 * 1024),
        cost_estimate=pl.CostEstimate(
            flops=2 * wout * T * 9 * C * C, bytes_accessed=2 << 20, transcendentals=0
        ),
    )(outer, acc, weights, gain)


def on_device(frames_in, norm_gain, conv_weight, conv_bias):
    section = lax.axis_index("section")
    tile = lax.axis_index("tile")
    tiles = lax.axis_size("tile")
    flip = tile % 2
    inner_pairs = [(i, i ^ 1) for i in range(tiles)]
    outer_pairs = [(i, i + 1) for i in range(1, tiles - 1, 2)]
    outer_pairs += [(i + 1, i) for i, _ in outer_pairs]
    same_core = [[i + c for i in range(0, tiles, 2)] for c in range(2)]

    padded = jnp.pad(frames_in, ((0, 0), (0, 0), (0, 0), (LAYERS, LAYERS)))
    strip = lax.dynamic_slice_in_dim(padded, section * STRIP, STRIP + 2 * LAYERS, axis=3)
    strip = jnp.pad(strip.transpose(2, 3, 0, 1), ((0, 0), (0, 0), (0, 0), (0, CP - C)))
    rows = [
        jnp.where(flip == 1, strip[2], strip[0]),
        strip[1],
        jnp.where(flip == 1, strip[0], strip[2]),
    ]

    small = jnp.concatenate(
        [three_parts(norm_gain[0]).reshape(-1), three_parts(conv_bias[0]).reshape(-1)]
    )
    small = jnp.pad(small, (0, SMALL * 128 - small.shape[0])).reshape(SMALL, 128)
    piece = jnp.concatenate([tap_piece(conv_weight[0], tile), small], axis=0)
    pieces = lax.all_to_all(
        jnp.broadcast_to(piece[None], (LAYERS,) + piece.shape), "section", 0, 0, tiled=True
    )
    parts = (
        pieces[:, PIECE:].astype(jnp.float32).reshape(LAYERS, SMALL * 128)[:, : 6 * C]
    ).reshape(LAYERS, 2, 3, C)
    vectors = parts[:, :, 0] + parts[:, :, 1] + parts[:, :, 2]
    vectors = jnp.pad(vectors, ((0, 0), (0, 0), (0, CP - C)))
    late = (lax.all_gather(pieces[FIRST:, :PIECE], "tile"),)
    first = jnp.broadcast_to(pieces[None, :FIRST, :PIECE], (tiles // 2, FIRST, PIECE, 128))
    mine = lax.all_to_all(first, "tile", 0, 0, axis_index_groups=same_core, tiled=True)
    theirs = lax.ppermute(mine, "tile", inner_pairs)
    early = (mine, theirs)

    inner = lax.ppermute(rows[2], "tile", inner_pairs)
    for layer in range(LAYERS):
        win = STRIP + 2 * (LAYERS - layer)
        outer = lax.ppermute(rows[0], "tile", outer_pairs)
        weights, which = (early, layer) if layer < FIRST else (late, layer - FIRST)
        if layer == FIRST:
            weights = (late[0][:, :1],)
        gain, bias = vectors[layer, 0:1], vectors[layer, 1:2]
        acc, row1, row2, w_outer = run_inner(win, which, rows, inner, weights, gain, bias)
        if layer + 1 < LAYERS:
            inner = lax.ppermute(row2, "tile", inner_pairs)
        row0 = run_outer(win, outer, acc, w_outer, gain)
        rows = [row0, row1, row2]

    share = T // LAYERS
    upper = jnp.where(flip == 1, rows[2], rows[0])
    lower = jnp.where(flip == 1, rows[0], rows[2])
    out = jnp.stack([row[:, :, :C] for row in (upper, rows[1], lower)])
    out = out.transpose(2, 0, 1, 3).reshape(LAYERS, share, 3, STRIP, C)
    out = lax.all_to_all(out, "section", 0, 0, tiled=True)
    return out.transpose(1, 4, 2, 0, 3).reshape(share, C, 3, LAYERS * STRIP)


def solution(mesh):
    placed = (
        P(None, None, "tile", None),
        P("section", None),
        P("section", None, None, None),
        P("section", None),
    )
    return jax.shard_map(
        on_device,
        mesh=mesh,
        in_specs=placed,
        out_specs=P("section", None, "tile", None),
        check_vma=False,
    )
```

```python
import functools

import jax
import jax.numpy as jnp
from jax import lax
from jax.experimental import pallas as pl
from jax.experimental.pallas import tpu as pltpu
from jax.sharding import PartitionSpec as P

LAYERS = 8
C = 192
CP = 256
T = 16
KT = 14 * 128
STRIP = 16
PIECE = 288
SMALL = 16
FIRST = 2
CH = 4


def tap_piece(weight, tile):
    tap = lax.dynamic_index_in_dim(weight, jnp.minimum(tile, 26), 0, keepdims=False).T
    low = tap[:, :128]
    high = jnp.concatenate([tap[: C // 2, 128:], tap[C // 2 :, 128:]], axis=1)
    return jnp.concatenate([low, high], axis=0)


def three_parts(vector):
    high = lax.reduce_precision(vector, 8, 7)
    rest = vector - high
    middle = lax.reduce_precision(rest, 8, 7)
    return jnp.stack([high, middle, rest - middle]).astype(jnp.bfloat16)


def unpack(flip, w_refs, wbuf):
    def piece(tap, rows):
        if len(w_refs) == 1:
            return w_refs[0][tap, rows, :]
        mine = lax.rem(tap, 2) == flip
        pick = [ref[lax.div(tap, 2), rows, :] for ref in w_refs]
        return jnp.where(mine, pick[0], pick[1])

    lane = lax.broadcasted_iota(jnp.int32, (C // 2, 128), 1)
    for b in range(3):
        b_at = b + flip * (2 - 2 * b)
        for e in range(3):
            full = (b * 3 + e) * 128
            half = (9 + e) * 128 + 64 * (b - 1) if b else 12 * 128 + 64 * e
            for a in range(3):
                tap = 9 * a + 3 * b_at + e
                high = piece(tap, slice(C, C + C // 2)).astype(jnp.float32)
                one = jnp.where(lane < 64, high, 0.0).astype(jnp.bfloat16)
                two = jnp.where(lane < 64, pltpu.roll(high, 64, 1), 0.0).astype(jnp.bfloat16)
                at = a * CP
                wbuf[full : full + 128, at : at + 128] = piece(tap, slice(0, 128))
                wbuf[half : half + 64, at : at + 128] = piece(tap, slice(128, C))
                wbuf[full : full + 96, at + 128 : at + CP] = one
                wbuf[full + 96 : full + 128, at + 128 : at + CP] = two[:32]
                wbuf[half : half + 64, at + 128 : at + CP] = two[32:]
    wbuf[KT - 64 : KT, :] = jnp.zeros((64, 3 * CP), jnp.bfloat16)


def normed(v, half_gain):
    v = v.astype(jnp.float32)
    ms = jnp.sum(v * v, axis=2, keepdims=True) * (1.0 / C)
    u = v * lax.rsqrt(ms + 1e-6) * half_gain
    return u + u * jnp.tanh(u)


def place_lone(buf, col, tile, value, moved):
    step = value.shape[0]
    buf[pl.ds(col + 2, step), :, tile * 128 : (tile + 1) * 128] = value
    before = buf[pl.ds(col + 1, step), :, tile * 128 : (tile + 1) * 128]
    lane = lax.broadcasted_iota(jnp.int32, before.shape, 2)
    buf[pl.ds(col + 1, step), :, tile * 128 : (tile + 1) * 128] = jnp.where(
        lane < 64, before, moved
    )
    buf[pl.ds(col, step), :, (tile + 1) * 128 : (tile + 2) * 128] = value


def time_summed(start, left, w_ref, lo, hi):
    wout = start.shape[0]
    time = lax.broadcasted_iota(jnp.int32, start.shape, 1)
    for a in range(3):
        part = jnp.dot(
            left, w_ref[lo:hi, a * CP : (a + 1) * CP], preferred_element_type=jnp.float32
        ).reshape(wout, T, CP)
        if a < 2:
            part = jnp.where(time >= 2 - a, pltpu.roll(part, 2 - a, 1), 0.0)
        start = start + part
    return start


def in_frame(value, first):
    where = first + lax.broadcasted_iota(jnp.int32, value.shape, 0)
    inside = jnp.logical_and(where >= 0, where < 128)
    return jnp.where(inside, value, 0.0).astype(jnp.bfloat16)


def inner_kernel(
    win, pieces, r0_ref, r1_ref, r2_ref, in_ref, gain_ref, bias_ref, *refs
):
    w_refs, (acc_ref, n1_ref, n2_ref, outer_ref, x9, wbuf) = refs[:pieces], refs[pieces:]
    wout = win - 2
    unpack(lax.axis_index("tile") % 2, w_refs, wbuf)
    outer_ref[0:384, :] = wbuf[0:384, :]
    outer_ref[384:640, :] = wbuf[12 * 128 : 14 * 128, :]
    gain = (0.5 * gain_ref[...]).reshape(1, 1, CP)

    for col in range(0, win, CH):
        step = min(CH, win - col)
        low, high, moved = [None], [None], [None]
        for ref in (r0_ref, r1_ref, r2_ref, in_ref):
            h = normed(ref[pl.ds(col, step)], gain)
            low.append(h[:, :, :128].astype(jnp.bfloat16))
            high.append(h[:, :, 128:])
            moved.append(pltpu.roll(h[:, :, 128:], 64, 2))
        for r in range(3):
            pair = (high[r + 1] + moved[r + 2]).astype(jnp.bfloat16)
            for e in range(3):
                at = pl.ds(col + 2 - e, step)
                for b in range(0 if r else 1, 3):
                    tile = b * 3 + e
                    x9[r, at, :, tile * 128 : (tile + 1) * 128] = low[r + b]
                x9[r, at, :, (9 + e) * 128 : (10 + e) * 128] = pair
            if r:
                place_lone(
                    x9.at[r], col, 12, high[r].astype(jnp.bfloat16), moved[r].astype(jnp.bfloat16)
                )

    bias = bias_ref[...].reshape(1, 1, CP)
    first = lax.axis_index("section") * STRIP + (STRIP - wout) // 2
    for row, src, out in ((1, r1_ref, n1_ref), (0, r0_ref, acc_ref), (2, r2_ref, n2_ref)):
        lo, hi = (0, KT) if row else (3 * 128, 12 * 128)
        left = x9[row, 2 : 2 + wout, :, lo:hi].reshape(wout * T, hi - lo)
        new = time_summed(src[1 : 1 + wout].astype(jnp.float32) + bias, left, wbuf, lo, hi)
        out[...] = in_frame(new, first) if row else new


def outer_kernel(win, out_ref, acc_ref, w_ref, gain_ref, n0_ref, x5):
    wout = win - 2
    gain = (0.5 * gain_ref[...]).reshape(1, 1, CP)

    for col in range(0, win, CH):
        step = min(CH, win - col)
        h = normed(out_ref[pl.ds(col, step)], gain)
        low = h[:, :, :128].astype(jnp.bfloat16)
        high = h[:, :, 128:]
        for e in range(3):
            x5[pl.ds(col + 2 - e, step), :, e * 128 : (e + 1) * 128] = low
        place_lone(
            x5, col, 3, high.astype(jnp.bfloat16), pltpu.roll(high, 64, 2).astype(jnp.bfloat16)
        )

    left = x5[2 : 2 + wout].reshape(wout * T, 640)
    first = lax.axis_index("section") * STRIP + (STRIP - wout) // 2
    n0_ref[...] = in_frame(time_summed(acc_ref[...], left, w_ref, 0, 640), first)


def run_inner(win, which, rows, inner, weights, gain, bias):
    wout = win - 2
    row_in = row_out = vector = pl.BlockSpec(memory_space=pltpu.VMEM)
    return pl.pallas_call(
        functools.partial(inner_kernel, win, len(weights)),
        grid=(1,),
        out_shape=[
            pltpu.VMEM((wout, T, CP), jnp.float32),
            jax.ShapeDtypeStruct((wout, T, CP), jnp.bfloat16),
            jax.ShapeDtypeStruct((wout, T, CP), jnp.bfloat16),
            pltpu.VMEM((640, 3 * CP), jnp.bfloat16),
        ],
        in_specs=[row_in] * 4
        + [vector] * 2
        + [
            pl.BlockSpec((w.shape[0], None, PIECE, 128), lambda i: (0, which, 0, 0))
            for w in weights
        ],
        out_specs=[row_out] * 3 + [row_out],
        scratch_shapes=[
            pltpu.VMEM((3, win + 2, T, KT), jnp.bfloat16),
            pltpu.VMEM((KT, 3 * CP), jnp.bfloat16),
        ],
        compiler_params=pltpu.CompilerParams(vmem_limit_bytes=22 * 1024 * 1024),
        cost_estimate=pl.CostEstimate(
            flops=4 * 3 * wout * T * 9 * 3 * C * C, bytes_accessed=4 << 20, transcendentals=0
        ),
    )(*rows, inner, gain, bias, *weights)


def run_outer(win, outer, acc, weights, gain):
    wout = win - 2
    return pl.pallas_call(
        functools.partial(outer_kernel, win),
        grid=(1,),
        out_shape=jax.ShapeDtypeStruct((wout, T, CP), jnp.bfloat16),
        in_specs=[
            pl.BlockSpec(memory_space=pltpu.VMEM),
            pl.BlockSpec(memory_space=pltpu.VMEM),
            pl.BlockSpec(memory_space=pltpu.VMEM),
            pl.BlockSpec(memory_space=pltpu.VMEM),
        ],
        out_specs=pl.BlockSpec(memory_space=pltpu.VMEM),
        scratch_shapes=[pltpu.VMEM((win + 2, T, 640), jnp.bfloat16)],
        compiler_params=pltpu.CompilerParams(vmem_limit_bytes=12 * 1024 * 1024),
        cost_estimate=pl.CostEstimate(
            flops=2 * wout * T * 9 * C * C, bytes_accessed=2 << 20, transcendentals=0
        ),
    )(outer, acc, weights, gain)


def on_device(frames_in, norm_gain, conv_weight, conv_bias):
    section = lax.axis_index("section")
    tile = lax.axis_index("tile")
    tiles = lax.axis_size("tile")
    flip = tile % 2
    inner_pairs = [(i, i ^ 1) for i in range(tiles)]
    outer_pairs = [(i, i + 1) for i in range(1, tiles - 1, 2)]
    outer_pairs += [(i + 1, i) for i, _ in outer_pairs]
    same_core = [[i + c for i in range(0, tiles, 2)] for c in range(2)]

    padded = jnp.pad(frames_in, ((0, 0), (0, 0), (0, 0), (LAYERS, LAYERS)))
    strip = lax.dynamic_slice_in_dim(padded, section * STRIP, STRIP + 2 * LAYERS, axis=3)
    strip = jnp.pad(strip.transpose(2, 3, 0, 1), ((0, 0), (0, 0), (0, 0), (0, CP - C)))
    rows = [
        jnp.where(flip == 1, strip[2], strip[0]),
        strip[1],
        jnp.where(flip == 1, strip[0], strip[2]),
    ]

    small = jnp.concatenate(
        [three_parts(norm_gain[0]).reshape(-1), three_parts(conv_bias[0]).reshape(-1)]
    )
    small = jnp.pad(small, (0, SMALL * 128 - small.shape[0])).reshape(SMALL, 128)
    piece = jnp.concatenate([tap_piece(conv_weight[0], tile), small], axis=0)
    pieces = lax.all_to_all(
        jnp.broadcast_to(piece[None], (LAYERS,) + piece.shape), "section", 0, 0, tiled=True
    )
    parts = (
        pieces[:, PIECE:].astype(jnp.float32).reshape(LAYERS, SMALL * 128)[:, : 6 * C]
    ).reshape(LAYERS, 2, 3, C)
    vectors = parts[:, :, 0] + parts[:, :, 1] + parts[:, :, 2]
    vectors = jnp.pad(vectors, ((0, 0), (0, 0), (0, CP - C)))
    late = (lax.all_gather(pieces[FIRST:, :PIECE], "tile"),)
    first = jnp.broadcast_to(pieces[None, :FIRST, :PIECE], (tiles // 2, FIRST, PIECE, 128))
    mine = lax.all_to_all(first, "tile", 0, 0, axis_index_groups=same_core, tiled=True)
    theirs = lax.ppermute(mine, "tile", inner_pairs)
    early = (mine, theirs)

    inner = lax.ppermute(rows[2], "tile", inner_pairs)
    for layer in range(LAYERS):
        win = STRIP + 2 * (LAYERS - layer)
        outer = lax.ppermute(rows[0], "tile", outer_pairs)
        weights, which = (early, layer) if layer < FIRST else (late, layer - FIRST)
        if layer == FIRST:
            weights = (late[0][:, :1],)
        gain, bias = vectors[layer, 0:1], vectors[layer, 1:2]
        acc, row1, row2, w_outer = run_inner(win, which, rows, inner, weights, gain, bias)
        if layer + 1 < LAYERS:
            inner = lax.ppermute(row2, "tile", inner_pairs)
        row0 = run_outer(win, outer, acc, w_outer, gain)
        rows = [row0, row1, row2]

    share = T // LAYERS
    upper = jnp.where(flip == 1, rows[2], rows[0])
    lower = jnp.where(flip == 1, rows[0], rows[2])
    out = jnp.stack([row[:, :, :C] for row in (upper, rows[1], lower)])
    out = out.transpose(2, 0, 1, 3).reshape(LAYERS, share, 3, STRIP, C)
    half = share * 3 * STRIP // 2
    flat = out.reshape(LAYERS, 2 * half, C)
    packed = jnp.concatenate([flat[:, :half], flat[:, half:]], axis=2)
    packed = lax.all_to_all(packed, "section", 0, 0, tiled=True)
    flat = jnp.concatenate([packed[:, :, :C], packed[:, :, C:]], axis=1)
    out = flat.reshape(LAYERS, share, 3, STRIP, C)
    return out.transpose(1, 4, 2, 0, 3).reshape(share, C, 3, LAYERS * STRIP)


def solution(mesh):
    placed = (
        P(None, None, "tile", None),
        P("section", None),
        P("section", None, None, None),
        P("section", None),
    )
    return jax.shard_map(
        on_device,
        mesh=mesh,
        in_specs=placed,
        out_specs=P("section", None, "tile", None),
        check_vma=False,
    )
```
